128 devices in a mesh: ctx: 16 (over y, x_hi, core), smp: 8 (over z, x_lo).
Axes of the slice: x: 4 (x_hi: 2, x_lo: 2; x = x_hi * 2 + x_lo), y: 4, z: 4, core: 2. Of those that a mesh axis runs over, the one named last changes fastest.
Arguments:
- prompt_input: bfloat16 [2048, 16384], P('smp', 'ctx'), may hold values from -6 to 6
- prompt_gate: bfloat16 [2048, 16384], P('smp', 'ctx'), may hold values from -6 to 6
- filters: float32 [2048, 16384], P('smp', 'ctx')
- skip: float32 [2048], replicated, may hold values from 0.2 to 1.8
- sample_input: bfloat16 [256, 1024, 2048], P(('ctx', 'smp')), may hold values from -6 to 6
- sample_gate: bfloat16 [256, 1024, 2048], P(('ctx', 'smp')), may hold values from -6 to 6
- lengths: int32 [256], P(('ctx', 'smp')), may hold values from 1 to 1024
Outputs:
- prompt_output: bfloat16 [2048, 16384], P('smp', 'ctx')
- sample_output: bfloat16 [256, 1024, 2048], P(('ctx', 'smp'))
The draws below stay inside these ranges and needn't reach their ends.
All inputs are finite; a program needn't handle non-finite values.
Results may differ from the reference program's by a relative error of at most 0.001.
Values sent between devices are 32-bit elements; how exact they have to be, the bound alone decides.
No kernel may reach another device: no remote copies, remote signals or barrier semaphores. Data moves between devices by JAX's collectives and lax.ppermute only.
A program may use at most 128 MiB of HBM per device.

```python
import jax
import jax.numpy as jnp

C = 2048
Q = 1024
PROMPT = 16384
SAMPLES = 256


def draw_filters(key, part):
    key = jax.random.fold_in(key, 11)
    rate_key, value_key = jax.random.split(key)
    low_rate = jnp.log(1.0 / (8.0 * PROMPT))
    high_rate = jnp.log(1.0 / 30.0)
    noise = jax.random.normal(value_key, (C, PROMPT), jnp.float32)
    rates = jnp.exp(jax.random.uniform(rate_key, (C, 1), jnp.float32, low_rate, high_rate))
    steps_along = jnp.arange(PROMPT, dtype=jnp.float32)[None, :]
    return (jnp.sqrt(2.0 * rates) * noise * jnp.exp(-rates * steps_along)).astype(jnp.float32)


def set_ends(result, stream_key, smallest, largest):
    place = [jax.random.randint(jax.random.fold_in(stream_key, axis), (), 0, length) for axis, length in enumerate(result.shape)]
    longest = result.shape.index(max(result.shape))
    neighbour = place[:longest] + [(place[longest] + 1) % result.shape[longest]] + place[longest + 1:]
    return result.at[tuple(place)].set(smallest).at[tuple(neighbour)].set(largest)


def shard_levels(stream_key, extent, cuts, smallest, top_value):
    level, own = 1.0, jax.random.fold_in(stream_key, 6)
    for dim, shards_of in cuts:
        heights = jnp.exp(jax.random.uniform(jax.random.fold_in(own, dim), (shards_of,), jnp.float32, smallest / len(cuts), top_value / len(cuts)))
        level = level * jnp.repeat(heights, extent[dim] // shards_of).reshape([-1 if axis == dim else 1 for axis in range(len(extent))])
    return level


def normal_values(stream_key, extent, deviation, most, pieces=(), held_as=jnp.bfloat16):
    values = deviation * jax.random.normal(stream_key, extent, jnp.float32)
    if pieces:
        values = values * shard_levels(stream_key, extent, pieces, -0.22, 0.18)
    return jnp.clip(values, -most, most).astype(held_as)


def setup_inputs(seed: int = 0) -> dict:
    seeds = jax.random.split(jax.random.key(seed), 8)
    return {
        "prompt_input": normal_values(seeds[0], (C, PROMPT), 1.0, 6.0, ((0, 8), (1, 16))),
        "prompt_gate": normal_values(seeds[1], (C, PROMPT), 1.0, 6.0, ((0, 8), (1, 16))),
        "filters": draw_filters(jax.random.fold_in(seeds[7], 71), 0),
        "skip": jnp.clip(jax.random.uniform(seeds[3], (C,), jnp.float32, 0.2, 1.8), 0.2, 1.8),
        "sample_input": normal_values(seeds[4], (SAMPLES, Q, C), 1.0, 6.0, ((0, 128),)),
        "sample_gate": normal_values(seeds[5], (SAMPLES, Q, C), 1.0, 6.0, ((0, 128),)),
        "lengths": set_ends(jax.random.randint(seeds[6], (SAMPLES,), 1, Q + 1), jax.random.fold_in(seeds[6], 1), 1, Q).astype(jnp.int32),
    }


def reference(prompt_input, prompt_gate, filters, skip, sample_input, sample_gate, lengths):
    signal = prompt_input.astype(jnp.float32)
    length_two = 2 * PROMPT
    spectrum = jnp.fft.rfft(signal, n=length_two, axis=1) * jnp.fft.rfft(filters, n=length_two, axis=1)
    convolved = jnp.fft.irfft(spectrum, n=length_two, axis=1)
    prompt_part = convolved[:, :PROMPT]
    prompt_output = (prompt_gate.astype(jnp.float32) * (prompt_part + skip[:, None] * signal)).astype(jnp.bfloat16)
    tail_state = convolved[:, PROMPT:PROMPT + Q]
    positions = jnp.arange(Q, dtype=jnp.int32)
    active = positions[None, :] < lengths[:, None]
    blended = sample_gate.astype(jnp.float32) * (tail_state.T[None, :, :] + skip[None, None, :] * sample_input.astype(jnp.float32))
    sample_output = jnp.where(active[:, :, None], blended, jnp.zeros_like(blended)).astype(jnp.bfloat16)
    return prompt_output, sample_output
```

```python
import functools

import jax
import jax.numpy as jnp
import numpy as np
from jax import lax
from jax.experimental import pallas as pl
from jax.experimental.pallas import tpu as pltpu
from jax.sharding import PartitionSpec as P

F32 = jnp.float32
BF16 = jnp.bfloat16
R = 128
ROWS = 8
SIDE = 4
AXES = ("ctx", "smp")

FIRST = ((1, 1, 1), (3, 3, 3), (2, 2, 2))
SECOND = ((2, 0, 0), (0, 2, 0), (0, 0, 2))
THIRD = ((1, 0, 0), (0, 1, 0), (0, 0, 1))
HELD_FIRST = ((0, 0, 0),) + FIRST
HELD_SECOND = tuple(
    tuple((a + b) % SIDE for a, b in zip(o, h)) for o in ((0, 0, 0),) + SECOND for h in HELD_FIRST
)


def chip_of(index):
    ctx, smp = divmod(index, 8)
    return ((ctx >> 1 & 1) * 2 + (smp & 1), ctx >> 2, smp >> 1, ctx & 1)


def index_of(x, y, z, core):
    x, y, z = x % SIDE, y % SIDE, z % SIDE
    return ((y * 2 + x // 2) * 2 + core) * 8 + z * 2 + x % 2


def take_from(array, offset, mirrored=False):
    pairs = []
    for index in range(2 * SIDE**3):
        x, y, z, core = chip_of(index)
        sign = -1 if mirrored and core else 1
        source = index_of(x + sign * offset[0], y + sign * offset[1], z + sign * offset[2], core)
        pairs.append((source, index))
    return lax.ppermute(array, AXES, pairs)


def swap_cores(array):
    pairs = []
    for index in range(2 * SIDE**3):
        x, y, z, core = chip_of(index)
        pairs.append((index, index_of(x, y, z, 1 - core)))
    return lax.ppermute(array, AXES, pairs)


def halves(values):
    high = values.astype(BF16)
    return high, (values - high.astype(F32)).astype(BF16)


def np_halves(values):
    values = np.asarray(values, np.float32)
    high = values.astype(jnp.bfloat16)
    low = (values - high.astype(np.float32)).astype(jnp.bfloat16)
    return high, low


@functools.cache
def tables():
    period = R * R
    r = np.arange(R)
    shifted = r + 0.25
    outer = 2 * np.pi * np.outer(shifted, r) / R
    first = np.concatenate([np.cos(outer), -np.sin(outer)], 0)
    inner = 2 * np.pi * (np.outer(r, r) % R) / R
    c, s = np.cos(inner), np.sin(inner)
    second = np.block([[c, -s], [s, c]])
    back = np.block([[c, s], [-s, c]])
    twist = 2 * np.pi * np.outer(shifted, r) / period
    turn = np.stack([np.cos(twist), np.sin(twist)]).astype(np.float32)
    real = np.concatenate([np.cos(outer.T), -np.sin(outer.T)], 1)
    tail = -np.concatenate([np.sin(outer.T), np.cos(outer.T)], 1)[:ROWS]
    last = np.concatenate([real, tail, np.zeros((ROWS, 2 * R))], 0)
    f_hi, f_lo = np_halves(first)
    l_hi, l_lo = np_halves(last)
    return (
        np.concatenate([f_hi, f_lo], 1),
        np.stack(np_halves(second)),
        np.stack(np_halves(back)),
        np.stack([l_hi, l_lo]),
        turn,
        (turn / period).astype(np.float32),
    )


def dot(left, right):
    return jnp.dot(left, right, preferred_element_type=F32)


def spread_kernel(signal_ref, filter_ref, out_ref):
    blocks, _, width = out_ref.shape[:3]
    for k in range(blocks):
        rows = pl.ds(k * width, width)
        for r in range(ROWS):
            cols = pl.ds(r * R, R)
            out_ref[k, 0, :, r, :] = signal_ref[rows, cols].astype(F32)
            out_ref[k, 1, :, r, :] = filter_ref[rows, cols]


def conv_kernel(
    base_ref, skip_ref, in_ref, first_ref, second_ref, back_ref, last_ref, turn_ref, unturn_ref, out_ref, tail_ref
):
    ctx_count = in_ref.shape[0]
    width = in_ref.shape[2]
    f_both = first_ref[...]
    f_hi = first_ref[:, :R]

    def two(pair, carry):
        chans = [2 * pair, 2 * pair + 1]
        signal = [in_ref[:, 0, c].reshape(R, R) for c in chans]
        taps = [in_ref[:, 1, c].reshape(R, R) for c in chans]
        x = jnp.concatenate(signal, 1).astype(BF16)
        h_hi, h_lo = halves(jnp.concatenate(taps, 1))
        xs = dot(f_both, jnp.concatenate([x, x], 0))
        hs = dot(f_both, jnp.concatenate([h_hi, h_hi], 0)) + dot(f_hi, h_lo)
        cos, sin = turn_ref[0], turn_ref[1]
        rows = []
        for spec in (xs, hs):
            for k in range(2):
                re, im = spec[:R, k * R : (k + 1) * R], spec[R:, k * R : (k + 1) * R]
                rows.append(jnp.concatenate([re * cos + im * sin, im * cos - re * sin], 1))
        hi, lo = halves(jnp.concatenate(rows, 0))
        spectra = dot(hi, second_ref[0]) + dot(lo, second_ref[0]) + dot(hi, second_ref[1])
        prods = []
        for k in range(2):
            xr, xi = spectra[k * R : (k + 1) * R, :R], spectra[k * R : (k + 1) * R, R:]
            hr, hi_ = spectra[(2 + k) * R : (3 + k) * R, :R], spectra[(2 + k) * R : (3 + k) * R, R:]
            prods.append(jnp.concatenate([xr * hr - xi * hi_, xr * hi_ + xi * hr], 1))
        hi, lo = halves(jnp.concatenate(prods, 0))
        timed = dot(hi, back_ref[0]) + dot(lo, back_ref[0]) + dot(hi, back_ref[1])
        cos, sin = unturn_ref[0], unturn_ref[1]
        cols = []
        for k in range(2):
            re, im = timed[k * R : (k + 1) * R, :R], timed[k * R : (k + 1) * R, R:]
            cols.append(jnp.concatenate([re * cos - im * sin, re * sin + im * cos], 0))
        hi, lo = halves(jnp.concatenate(cols, 1))
        result = dot(last_ref[0], hi) + dot(last_ref[0], lo) + dot(last_ref[1], hi)
        for k in range(2):
            skip = skip_ref[base_ref[0] + chans[k]]
            conv = result[:R, k * R : (k + 1) * R] + skip * signal[k]
            out_ref[:, chans[k]] = conv.reshape(ctx_count, ROWS, R)
            tail_ref[chans[k]] = result[R : R + ROWS, k * R : (k + 1) * R]
        return carry

    lax.fori_loop(0, width // 2, two, 0)


def finish_kernel(conv_ref, gate_ref, out_ref):
    blocks, width = conv_ref.shape[:2]
    for k in range(blocks):
        rows = pl.ds(k * width, width)
        for r in range(ROWS):
            cols = pl.ds(r * R, R)
            out_ref[rows, cols] = (gate_ref[rows, cols].astype(F32) * conv_ref[k, :, r, :]).astype(BF16)


def sample_kernel(
    place_ref, lengths_ref, skip_ref, input_ref, gate_ref, *rest
):
    pieces, (out_ref, tail_ref, sem) = rest[:8], rest[8:]
    step = pl.program_id(0)
    width = 16

    @pl.when(step == 0)
    def _():
        for array, piece_ref in enumerate(pieces):
            other, part = divmod(array, 4)
            core = place_ref[3] if other == 0 else 1 - place_ref[3]
            sign = 1 - 2 * core
            extra = (0, 0, 0) if part == 0 else THIRD[part - 1]
            for slot, held in enumerate(HELD_SECOND):
                x, y, z = [
                    (place_ref[i] + held[i] + sign * extra[i] + SIDE) % SIDE for i in range(3)
                ]
                channel = (z * 2 + x % 2) * 256 + core * 128 + (y * 2 + x // 2) * width
                copy = pltpu.make_async_copy(
                    piece_ref.at[pl.ds(slot * width, width)],
                    tail_ref.at[pl.ds(pl.multiple_of(channel, width), width)],
                    sem,
                )
                copy.start()
        pltpu.make_async_copy(tail_ref, tail_ref, sem).wait()

    positions = step * R + lax.broadcasted_iota(jnp.int32, (R, 1), 0)
    for block in range(tail_ref.shape[0] // R):
        cols = pl.ds(block * R, R)
        state = tail_ref[cols, step, :].T
        for i in range(input_ref.shape[0]):
            blended = gate_ref[i, :, cols].astype(F32) * (
                state + skip_ref[:, cols] * input_ref[i, :, cols].astype(F32)
            )
            out_ref[i, :, cols] = jnp.where(positions < lengths_ref[i], blended, 0.0).astype(BF16)


VMEM = pl.BlockSpec(memory_space=pltpu.VMEM)
SMEM = pl.BlockSpec(memory_space=pltpu.SMEM)


def on_device(prompt_input, prompt_gate, filters, skip, sample_input, sample_gate, lengths):
    width_dev, span = prompt_input.shape
    ctx_count = 16
    width = width_dev // ctx_count
    ctx, smp = lax.axis_index("ctx"), lax.axis_index("smp")
    core = ctx % 2
    place = jnp.stack([(ctx // 2 % 2) * 2 + smp % 2, ctx // 4, smp // 2, core]).astype(jnp.int32)
    base = (smp * width_dev + (core * 8 + ctx // 2) * width).astype(jnp.int32).reshape(1)

    spread = pl.pallas_call(
        spread_kernel,
        grid=(ctx_count,),
        in_specs=[pl.BlockSpec((width, span), lambda k: (k % 2 * 8 + k // 2, 0))] * 2,
        out_specs=pl.BlockSpec((1, 2, width, ROWS, R), lambda k: (k, 0, 0, 0, 0)),
        out_shape=jax.ShapeDtypeStruct((ctx_count, 2, width, ROWS, R), F32),
        name="spread",
    )(prompt_input, filters)
    regrouped = lax.all_to_all(spread, "ctx", split_axis=0, concat_axis=0, tiled=True)

    convolved, tail = pl.pallas_call(
        conv_kernel,
        in_specs=[SMEM, SMEM] + [VMEM] * 7,
        out_specs=[VMEM, VMEM],
        out_shape=[
            jax.ShapeDtypeStruct((ctx_count, width, ROWS, R), F32),
            jax.ShapeDtypeStruct((width, ROWS, R), F32),
        ],
        compiler_params=pltpu.CompilerParams(vmem_limit_bytes=40 * 2**20),
        name="conv",
    )(base, skip, regrouped, *tables())

    held = jnp.concatenate([tail] + [take_from(tail, o) for o in FIRST], 0)
    held = jnp.concatenate([held] + [take_from(held, o) for o in SECOND], 0)
    mine = [held] + [take_from(held, o, mirrored=True) for o in THIRD]
    other = [swap_cores(part) for part in mine]

    returned = lax.all_to_all(convolved, "ctx", split_axis=0, concat_axis=0, tiled=True)
    prompt_output = pl.pallas_call(
        finish_kernel,
        grid=(ctx_count,),
        in_specs=[
            pl.BlockSpec((1, width, ROWS, R), lambda k: (k, 0, 0, 0)),
            pl.BlockSpec((width, span), lambda k: (k % 2 * 8 + k // 2, 0)),
        ],
        out_specs=pl.BlockSpec((width, span), lambda k: (k % 2 * 8 + k // 2, 0)),
        out_shape=jax.ShapeDtypeStruct((width_dev, span), BF16),
        name="finish",
    )(returned, prompt_gate)

    local, length, channels = sample_input.shape
    block = pl.BlockSpec((local, R, channels), lambda j: (0, j, 0))
    sample_output = pl.pallas_call(
        sample_kernel,
        grid=(length // R,),
        in_specs=[SMEM, SMEM, pl.BlockSpec((1, channels), lambda j: (0, 0)), block, block]
        + [pl.BlockSpec(memory_space=pl.ANY)] * 8,
        out_specs=block,
        out_shape=jax.ShapeDtypeStruct(sample_input.shape, BF16),
        scratch_shapes=[
            pltpu.VMEM((channels, ROWS, R), F32),
            pltpu.SemaphoreType.DMA,
        ],
        compiler_params=pltpu.CompilerParams(vmem_limit_bytes=40 * 2**20),
        name="samples",
    )(place, lengths, skip.reshape(1, channels), sample_input, sample_gate, *mine, *other)
    return prompt_output, sample_output


def solution(mesh):
    return jax.shard_map(
        on_device,
        mesh=mesh,
        in_specs=(
            P("smp", "ctx"),
            P("smp", "ctx"),
            P("smp", "ctx"),
            P(),
            P(("ctx", "smp"), None, None),
            P(("ctx", "smp"), None, None),
            P(("ctx", "smp")),
        ),
        out_specs=(P("smp", "ctx"), P(("ctx", "smp"), None, None)),
        check_vma=False,
    )
```

```python
import functools

import jax
import jax.numpy as jnp
import numpy as np
from jax import lax
from jax.experimental import pallas as pl
from jax.experimental.pallas import tpu as pltpu
from jax.sharding import PartitionSpec as P

F32 = jnp.float32
BF16 = jnp.bfloat16
R = 128
ROWS = 8
SIDE = 4
AXES = ("ctx", "smp")

FIRST = ((1, 1, 1), (3, 3, 3), (2, 2, 2))
SECOND = ((2, 0, 0), (0, 2, 0), (0, 0, 2))
THIRD = ((1, 0, 0), (0, 1, 0), (0, 0, 1))
HELD_FIRST = ((0, 0, 0),) + FIRST
HELD_SECOND = tuple(
    tuple((a + b) % SIDE for a, b in zip(o, h)) for o in ((0, 0, 0),) + SECOND for h in HELD_FIRST
)


def chip_of(index):
    ctx, smp = divmod(index, 8)
    return ((ctx >> 1 & 1) * 2 + (smp & 1), ctx >> 2, smp >> 1, ctx & 1)


def index_of(x, y, z, core):
    x, y, z = x % SIDE, y % SIDE, z % SIDE
    return ((y * 2 + x // 2) * 2 + core) * 8 + z * 2 + x % 2


def take_from(array, offset, mirrored=False):
    pairs = []
    for index in range(2 * SIDE**3):
        x, y, z, core = chip_of(index)
        sign = -1 if mirrored and core else 1
        source = index_of(x + sign * offset[0], y + sign * offset[1], z + sign * offset[2], core)
        pairs.append((source, index))
    return lax.ppermute(array, AXES, pairs)


def swap_cores(array):
    pairs = []
    for index in range(2 * SIDE**3):
        x, y, z, core = chip_of(index)
        pairs.append((index, index_of(x, y, z, 1 - core)))
    return lax.ppermute(array, AXES, pairs)


def halves(values):
    high = values.astype(BF16)
    return high, (values - high.astype(F32)).astype(BF16)


def np_halves(values):
    values = np.asarray(values, np.float32)
    high = values.astype(jnp.bfloat16)
    low = (values - high.astype(np.float32)).astype(jnp.bfloat16)
    return high, low


@functools.cache
def tables():
    period = R * R
    r = np.arange(R)
    shifted = r + 0.25
    outer = 2 * np.pi * np.outer(shifted, r) / R
    first = np.concatenate([np.cos(outer), -np.sin(outer)], 0)
    inner = 2 * np.pi * (np.outer(r, r) % R) / R
    c, s = np.cos(inner), np.sin(inner)
    second = np.block([[c, -s], [s, c]])
    back = np.block([[c, s], [-s, c]])
    twist = 2 * np.pi * np.outer(shifted, r) / period
    turn = np.stack([np.cos(twist), np.sin(twist)]).astype(np.float32)
    real = np.concatenate([np.cos(outer.T), -np.sin(outer.T)], 1)
    tail = -np.concatenate([np.sin(outer.T), np.cos(outer.T)], 1)[:ROWS]
    last = np.concatenate([real, tail, np.zeros((ROWS, 2 * R))], 0)
    f_hi, f_lo = np_halves(first)
    l_hi, l_lo = np_halves(last)
    return (
        np.concatenate([f_hi, f_lo], 1),
        np.stack(np_halves(second)),
        np.stack(np_halves(back)),
        np.stack([l_hi, l_lo]),
        turn,
        (turn / period).astype(np.float32),
    )


@functools.cache
def arrivals():
    table = np.zeros((2 * SIDE**3, 8 * 16), np.int32)
    for index in range(2 * SIDE**3):
        own = chip_of(index)
        for array in range(8):
            core = own[3] ^ (array // 4)
            extra = ((0, 0, 0),) + THIRD
            for slot, held in enumerate(HELD_SECOND):
                sign = -1 if core else 1
                x, y, z = [(own[i] + held[i] + sign * extra[array % 4][i]) % SIDE for i in range(3)]
                table[index, array * 16 + slot] = (z * 2 + x % 2) * 256 + core * 128 + (y * 2 + x // 2) * 16
    return table


def dot(left, right):
    return jnp.dot(left, right, preferred_element_type=F32)


WIDTH = 16


def spread_kernel(signal_ref, filter_ref, out_ref):
    for k in range(out_ref.shape[0]):
        rows = pl.ds(k * WIDTH, WIDTH)
        out_ref[k, 0, 0] = signal_ref[rows, :].astype(F32).reshape(WIDTH, ROWS, R)
        out_ref[k, 0, 1] = filter_ref[rows, :].reshape(WIDTH, ROWS, R)


def conv_kernel(base_ref, skip_ref, in_hbm, *refs):
    consts, (out_hbm, tail_ref), refs = refs[:6], refs[6:8], refs[8:]
    (in_ref, out_ref), held, (in_sem, table_sem, out_sem) = refs[:2], refs[2:8], refs[8:]
    first_ref, second_ref, back_ref, last_ref, turn_ref, unturn_ref = held
    ctx_count = in_hbm.shape[0]
    group = in_ref.shape[2] // in_sem.shape[0]
    parts = range(in_sem.shape[0])

    def fetch(part):
        chans = pl.ds(part * group, group)
        return pltpu.make_async_copy(in_hbm.at[:, :, chans], in_ref.at[:, :, chans], in_sem.at[part])

    def leave(part):
        chans = pl.ds(part * group, group)
        return pltpu.make_async_copy(out_ref.at[:, chans], out_hbm.at[:, chans], out_sem.at[part])

    loads = [pltpu.make_async_copy(a, b, table_sem.at[i]) for i, (a, b) in enumerate(zip(consts, held))]
    fetch(0).start()
    for load in loads:
        load.start()
    for part in parts[1:]:
        fetch(part).start()
    for load in loads:
        load.wait()
    f_both = first_ref[...]
    f_hi = first_ref[:, :R]

    for part in parts:
        fetch(part).wait()
        chans = [part * group + k for k in range(group)]
        signal = [in_ref[:, 0, c].reshape(R, R) for c in chans]
        taps = [in_ref[:, 1, c].reshape(R, R) for c in chans]
        x = jnp.concatenate(signal, 1).astype(BF16)
        h_hi, h_lo = halves(jnp.concatenate(taps, 1))
        xs = dot(f_both, jnp.concatenate([x, x], 0))
        hs = dot(f_both, jnp.concatenate([h_hi, h_hi], 0)) + dot(f_hi, h_lo)
        cos, sin = turn_ref[0], turn_ref[1]
        rows = []
        for spec in (xs, hs):
            for k in range(group):
                re, im = spec[:R, k * R : (k + 1) * R], spec[R:, k * R : (k + 1) * R]
                rows.append(jnp.concatenate([re * cos + im * sin, im * cos - re * sin], 1))
        hi, lo = halves(jnp.concatenate(rows, 0))
        spectra = dot(hi, second_ref[0]) + dot(lo, second_ref[0]) + dot(hi, second_ref[1])
        prods = []
        for k in range(group):
            xr, xi = spectra[k * R : (k + 1) * R, :R], spectra[k * R : (k + 1) * R, R:]
            other = group + k
            hr, hq = spectra[other * R : (other + 1) * R, :R], spectra[other * R : (other + 1) * R, R:]
            prods.append(jnp.concatenate([xr * hr - xi * hq, xr * hq + xi * hr], 1))
        hi, lo = halves(jnp.concatenate(prods, 0))
        timed = dot(hi, back_ref[0]) + dot(lo, back_ref[0]) + dot(hi, back_ref[1])
        cos, sin = unturn_ref[0], unturn_ref[1]
        cols = []
        for k in range(group):
            re, im = timed[k * R : (k + 1) * R, :R], timed[k * R : (k + 1) * R, R:]
            cols.append(jnp.concatenate([re * cos - im * sin, re * sin + im * cos], 0))
        hi, lo = halves(jnp.concatenate(cols, 1))
        result = dot(last_ref[0], hi) + dot(last_ref[0], lo) + dot(last_ref[1], hi)
        for k in range(group):
            skip = skip_ref[base_ref[0] + chans[k]]
            conv = result[:R, k * R : (k + 1) * R] + skip * signal[k]
            out_ref[:, chans[k]] = conv.reshape(ctx_count, ROWS, R)
            tail_ref[:, chans[k], :] = result[R : R + ROWS, k * R : (k + 1) * R]
        leave(part).start()
    for part in parts:
        leave(part).wait()


def finish_kernel(after_ref, conv_ref, gate_ref, out_ref):
    for k in range(conv_ref.shape[0]):
        rows = pl.ds(k * WIDTH, WIDTH)
        conv = conv_ref[k, 0].reshape(WIDTH, ROWS * R)
        out_ref[rows, :] = (gate_ref[rows, :].astype(F32) * conv).astype(BF16)


def sample_kernel(place_ref, lengths_ref, skip_ref, input_ref, gate_ref, *rest):
    pieces, (out_ref, done_ref, tail_ref, sem) = rest[:8], rest[8:]
    step = pl.program_id(0)

    @pl.when(step == 0)
    def _():
        done_ref[...] = jnp.zeros_like(done_ref)
        for array, piece_ref in enumerate(pieces):
            for slot in range(16):
                channel = pl.multiple_of(place_ref[array * 16 + slot], WIDTH)
                pltpu.make_async_copy(piece_ref.at[slot], tail_ref.at[:, pl.ds(channel, WIDTH)], sem).start()
        pltpu.make_async_copy(tail_ref, tail_ref, sem).wait()

    positions = step * R + lax.broadcasted_iota(jnp.int32, (R, R), 0)
    for block in range(tail_ref.shape[1] // R):
        cols = pl.ds(block * R, R)
        state = tail_ref[step, cols, :].T
        for i in range(input_ref.shape[0]):
            blended = gate_ref[i, :, cols].astype(F32) * (
                state + skip_ref[:, cols] * input_ref[i, :, cols].astype(F32)
            )
            out_ref[i, :, cols] = jnp.where(positions < lengths_ref[i], blended, 0.0).astype(BF16)


VMEM = pl.BlockSpec(memory_space=pltpu.VMEM)
SMEM = pl.BlockSpec(memory_space=pltpu.SMEM)
ANY = pl.BlockSpec(memory_space=pl.ANY)


def on_device(prompt_input, prompt_gate, filters, skip, sample_input, sample_gate, lengths):
    width_dev, span = prompt_input.shape
    ctx_count = 16
    half = ctx_count // 2
    ctx, smp = lax.axis_index("ctx"), lax.axis_index("smp")
    place = lax.dynamic_index_in_dim(jnp.asarray(arrivals()), ctx * 8 + smp, keepdims=False)
    base = (smp * width_dev + (ctx % 2 * half + ctx // 2) * WIDTH).astype(jnp.int32).reshape(1)

    spread = pl.pallas_call(
        spread_kernel,
        grid=(2,),
        in_specs=[pl.BlockSpec((width_dev // 2, span), lambda k: (k, 0))] * 2,
        out_specs=pl.BlockSpec((half, 1, 2, WIDTH, ROWS, R), lambda k: (0, k, 0, 0, 0, 0)),
        out_shape=jax.ShapeDtypeStruct((half, 2, 2, WIDTH, ROWS, R), F32),
        name="spread",
    )(prompt_input, filters)
    spread = spread.reshape(ctx_count, 2, WIDTH, ROWS, R)
    regrouped = lax.all_to_all(spread, "ctx", split_axis=0, concat_axis=0, tiled=True)

    consts = [jnp.asarray(table) for table in tables()]
    parts = 2
    convolved, tail = pl.pallas_call(
        conv_kernel,
        in_specs=[SMEM, SMEM] + [ANY] * 7,
        out_specs=[ANY, VMEM],
        out_shape=[
            jax.ShapeDtypeStruct((ctx_count, WIDTH, ROWS, R), F32),
            jax.ShapeDtypeStruct((ROWS, WIDTH, R), F32),
        ],
        scratch_shapes=[
            pltpu.VMEM(regrouped.shape, F32),
            pltpu.VMEM((ctx_count, WIDTH, ROWS, R), F32),
            *[pltpu.VMEM(table.shape, table.dtype) for table in consts],
            pltpu.SemaphoreType.DMA((parts,)),
            pltpu.SemaphoreType.DMA((len(consts),)),
            pltpu.SemaphoreType.DMA((parts,)),
        ],
        compiler_params=pltpu.CompilerParams(vmem_limit_bytes=56 * 2**20),
        name="conv",
    )(base, skip, regrouped, *consts)

    tail = tail[None]
    held = jnp.concatenate([tail] + [take_from(tail, o) for o in FIRST], 0)
    held = jnp.concatenate([held] + [take_from(held, o) for o in SECOND], 0)
    mine = [held] + [take_from(held, o, mirrored=True) for o in THIRD]
    other = [swap_cores(part) for part in mine]

    local, length, channels = sample_input.shape
    block = pl.BlockSpec((local, R, channels), lambda j: (0, j, 0))
    sample_output, done = pl.pallas_call(
        sample_kernel,
        grid=(length // R,),
        in_specs=[SMEM, SMEM, pl.BlockSpec((1, channels), lambda j: (0, 0)), block, block] + [ANY] * 8,
        out_specs=[block, pl.BlockSpec((8, R), lambda j: (0, 0))],
        out_shape=[jax.ShapeDtypeStruct(sample_input.shape, BF16), jax.ShapeDtypeStruct((8, R), F32)],
        scratch_shapes=[pltpu.VMEM((ROWS, channels, R), F32), pltpu.SemaphoreType.DMA],
        compiler_params=pltpu.CompilerParams(vmem_limit_bytes=56 * 2**20),
        name="samples",
    )(place, lengths, skip.reshape(1, channels), sample_input, sample_gate, *mine, *other)

    returned = lax.all_to_all(convolved, "ctx", split_axis=0, concat_axis=0, tiled=True)
    prompt_output = pl.pallas_call(
        finish_kernel,
        grid=(2,),
        in_specs=[
            ANY,
            pl.BlockSpec((half, 1, WIDTH, ROWS, R), lambda k: (0, k, 0, 0, 0)),
            pl.BlockSpec((width_dev // 2, span), lambda k: (k, 0)),
        ],
        out_specs=pl.BlockSpec((width_dev // 2, span), lambda k: (k, 0)),
        out_shape=jax.ShapeDtypeStruct((width_dev, span), BF16),
        name="finish",
    )(done, returned.reshape(half, 2, WIDTH, ROWS, R), prompt_gate)
    return prompt_output, sample_output


def solution(mesh):
    return jax.shard_map(
        on_device,
        mesh=mesh,
        in_specs=(
            P("smp", "ctx"),
            P("smp", "ctx"),
            P("smp", "ctx"),
            P(),
            P(("ctx", "smp"), None, None),
            P(("ctx", "smp"), None, None),
            P(("ctx", "smp")),
        ),
        out_specs=(P("smp", "ctx"), P(("ctx", "smp"), None, None)),
        check_vma=False,
    )
```

```python
import functools

import jax
import jax.numpy as jnp
import numpy as np
from jax import lax
from jax.experimental import pallas as pl
from jax.experimental.pallas import tpu as pltpu
from jax.sharding import PartitionSpec as P

F32 = jnp.float32
BF16 = jnp.bfloat16
R = 128
ROWS = 8
SIDE = 4
AXES = ("ctx", "smp")

FIRST = ((1, 1, 1), (3, 3, 3), (2, 2, 2))
SECOND = ((2, 0, 0), (0, 2, 0), (0, 0, 2))
THIRD = ((1, 0, 0), (0, 1, 0), (0, 0, 1))
HELD_FIRST = ((0, 0, 0),) + FIRST
HELD_SECOND = tuple(
    tuple((a + b) % SIDE for a, b in zip(o, h)) for o in ((0, 0, 0),) + SECOND for h in HELD_FIRST
)


def chip_of(index):
    ctx, smp = divmod(index, 8)
    return ((ctx >> 1 & 1) * 2 + (smp & 1), ctx >> 2, smp >> 1, ctx & 1)


def index_of(x, y, z, core):
    x, y, z = x % SIDE, y % SIDE, z % SIDE
    return ((y * 2 + x // 2) * 2 + core) * 8 + z * 2 + x % 2


def take_from(array, offset, mirrored=False):
    pairs = []
    for index in range(2 * SIDE**3):
        x, y, z, core = chip_of(index)
        sign = -1 if mirrored and core else 1
        source = index_of(x + sign * offset[0], y + sign * offset[1], z + sign * offset[2], core)
        pairs.append((source, index))
    return lax.ppermute(array, AXES, pairs)


def swap_cores(array):
    pairs = []
    for index in range(2 * SIDE**3):
        x, y, z, core = chip_of(index)
        pairs.append((index, index_of(x, y, z, 1 - core)))
    return lax.ppermute(array, AXES, pairs)


def halves(values):
    high = values.astype(BF16)
    return high, (values - high.astype(F32)).astype(BF16)


def np_halves(values):
    values = np.asarray(values, np.float32)
    high = values.astype(jnp.bfloat16)
    low = (values - high.astype(np.float32)).astype(jnp.bfloat16)
    return high, low


@functools.cache
def tables():
    period = R * R
    r = np.arange(R)
    shifted = r + 0.25
    outer = 2 * np.pi * np.outer(shifted, r) / R
    first = np.concatenate([np.cos(outer), -np.sin(outer)], 0)
    inner = 2 * np.pi * (np.outer(r, r) % R) / R
    c, s = np.cos(inner), np.sin(inner)
    second = np.block([[c, -s], [s, c]])
    back = np.block([[c, s], [-s, c]])
    twist = 2 * np.pi * np.outer(shifted, r) / period
    turn = np.stack([np.cos(twist), np.sin(twist)]).astype(np.float32)
    real = np.concatenate([np.cos(outer.T), -np.sin(outer.T)], 1)
    tail = -np.concatenate([np.sin(outer.T), np.cos(outer.T)], 1)[:ROWS]
    last = np.concatenate([real, tail, np.zeros((ROWS, 2 * R))], 0)
    f_hi, f_lo = np_halves(first)
    l_hi, l_lo = np_halves(last / period)
    return (
        np.concatenate([f_hi, f_lo], 1),
        np.stack(np_halves(second)),
        np.stack(np_halves(back)),
        np.stack([l_hi, l_lo]),
        turn,
    )


@functools.cache
def arrivals():
    table = np.zeros((2 * SIDE**3, 8 * 16), np.int32)
    for index in range(2 * SIDE**3):
        own = chip_of(index)
        for array in range(8):
            core = own[3] ^ (array // 4)
            extra = ((0, 0, 0),) + THIRD
            for slot, held in enumerate(HELD_SECOND):
                sign = -1 if core else 1
                x, y, z = [(own[i] + held[i] + sign * extra[array % 4][i]) % SIDE for i in range(3)]
                table[index, array * 16 + slot] = (z * 2 + x % 2) * 256 + core * 128 + (y * 2 + x // 2) * 16
    return table


def dot(left, right):
    return jnp.dot(left, right, preferred_element_type=F32)


WIDTH = 16
GROUP = 2


def spread_kernel(signal_ref, filter_ref, out_ref):
    for k in range(out_ref.shape[0]):
        rows = pl.ds(k * WIDTH, WIDTH)
        out_ref[k, 0, 0] = signal_ref[rows, :].astype(F32).reshape(WIDTH, ROWS, R)
        out_ref[k, 0, 1] = filter_ref[rows, :].reshape(WIDTH, ROWS, R)


def conv_kernel(base_ref, place_ref, in_ref, skip_hbm, *refs):
    first_ref, second_ref, back_ref, last_ref, turn_ref = refs[:5]
    out_hbm, tail_ref, skip_ref, out_ref, skip_sem, out_sem = refs[-6:]
    ctx_count = in_ref.shape[0]
    parts = in_ref.shape[2] // GROUP
    load = pltpu.make_async_copy(skip_hbm, skip_ref, skip_sem)
    load.start()
    load.wait()
    f_both = first_ref[...]
    f_hi = first_ref[:, :R]

    def chans(part):
        return [part * GROUP + k for k in range(GROUP)]

    def columns(part):
        signal = [in_ref[:, 0, c].reshape(R, R) for c in chans(part)]
        taps = [in_ref[:, 1, c].reshape(R, R) for c in chans(part)]
        x = jnp.concatenate(signal, 1).astype(BF16)
        h_hi, h_lo = halves(jnp.concatenate(taps, 1))
        xs = dot(f_both, jnp.concatenate([x, x], 0))
        hs = dot(f_both, jnp.concatenate([h_hi, h_hi], 0)) + dot(f_hi, h_lo)
        cos, sin = turn_ref[0], turn_ref[1]
        rows = []
        for spec in (xs, hs):
            for k in range(GROUP):
                re, im = spec[:R, k * R : (k + 1) * R], spec[R:, k * R : (k + 1) * R]
                rows.append(jnp.concatenate([re * cos + im * sin, im * cos - re * sin], 1))
        return halves(jnp.concatenate(rows, 0))

    def product(part, value):
        hi, lo = value
        spectra = dot(hi, second_ref[0]) + dot(lo, second_ref[0]) + dot(hi, second_ref[1])
        prods = []
        for k in range(GROUP):
            xr, xi = spectra[k * R : (k + 1) * R, :R], spectra[k * R : (k + 1) * R, R:]
            other = GROUP + k
            hr, hq = spectra[other * R : (other + 1) * R, :R], spectra[other * R : (other + 1) * R, R:]
            prods.append(jnp.concatenate([xr * hr - xi * hq, xr * hq + xi * hr], 1))
        return halves(jnp.concatenate(prods, 0))

    def returning(part, value):
        hi, lo = value
        timed = dot(hi, back_ref[0]) + dot(lo, back_ref[0]) + dot(hi, back_ref[1])
        cos, sin = turn_ref[0], turn_ref[1]
        cols = []
        for k in range(GROUP):
            re, im = timed[k * R : (k + 1) * R, :R], timed[k * R : (k + 1) * R, R:]
            cols.append(jnp.concatenate([re * cos - im * sin, re * sin + im * cos], 0))
        return halves(jnp.concatenate(cols, 1))

    def positions(part, value):
        hi, lo = value
        result = dot(last_ref[0], hi) + dot(last_ref[0], lo) + dot(last_ref[1], hi)
        for k, c in enumerate(chans(part)):
            conv = result[:R, k * R : (k + 1) * R] + skip_ref[base_ref[0] + c] * in_ref[:, 0, c].reshape(R, R)
            out_ref[:, c] = conv.reshape(ctx_count, ROWS, R)
            tail_ref[:, c, :] = result[R : R + ROWS, k * R : (k + 1) * R]

    values = {}
    for step in range(parts + 3):
        for stage, section in ((3, positions), (2, returning), (1, product), (0, columns)):
            part = step - stage
            if 0 <= part < parts:
                values[part] = section(part, values[part]) if stage else section(part)
    leave = pltpu.make_async_copy(out_ref, out_hbm, out_sem)
    leave.start()
    leave.wait()


def finish_kernel(after_ref, conv_ref, gate_ref, out_ref):
    for k in range(conv_ref.shape[0]):
        rows = pl.ds(k * WIDTH, WIDTH)
        conv = conv_ref[k, 0].reshape(WIDTH, ROWS * R)
        out_ref[rows, :] = (gate_ref[rows, :].astype(F32) * conv).astype(BF16)


def hold_kernel(after_ref, *refs):
    count = len(refs) // 2
    copies = [pltpu.make_async_copy(refs[i], refs[count + i], refs[-1].at[i]) for i in range(count)]
    for copy in copies:
        copy.start()
    for copy in copies:
        copy.wait()


def sample_kernel(place_ref, lengths_ref, skip_ref, input_ref, gate_ref, *rest):
    pieces, (out_ref, done_ref, tail_ref, sem) = rest[:8], rest[8:]
    step = pl.program_id(0)

    @pl.when(step == 0)
    def _():
        done_ref[...] = jnp.zeros_like(done_ref)
        for array, piece_ref in enumerate(pieces):
            for slot in range(16):
                channel = pl.multiple_of(place_ref[array * 16 + slot], WIDTH)
                pltpu.make_async_copy(piece_ref.at[slot], tail_ref.at[:, pl.ds(channel, WIDTH)], sem).start()
        pltpu.make_async_copy(tail_ref, tail_ref, sem).wait()

    positions = step * R + lax.broadcasted_iota(jnp.int32, (R, R), 0)
    for block in range(tail_ref.shape[1] // R):
        cols = pl.ds(block * R, R)
        state = tail_ref[step, cols, :].T
        for i in range(input_ref.shape[0]):
            blended = gate_ref[i, :, cols].astype(F32) * (
                state + skip_ref[:, cols] * input_ref[i, :, cols].astype(F32)
            )
            out_ref[i, :, cols] = jnp.where(positions < lengths_ref[i], blended, 0.0).astype(BF16)


VMEM = pl.BlockSpec(memory_space=pltpu.VMEM)
SMEM = pl.BlockSpec(memory_space=pltpu.SMEM)
ANY = pl.BlockSpec(memory_space=pl.ANY)


def on_device(prompt_input, prompt_gate, filters, skip, sample_input, sample_gate, lengths):
    width_dev, span = prompt_input.shape
    ctx_count = 16
    half = ctx_count // 2
    ctx, smp = lax.axis_index("ctx"), lax.axis_index("smp")
    place = lax.dynamic_index_in_dim(jnp.asarray(arrivals()), ctx * 8 + smp, keepdims=False)
    base = (smp * width_dev + (ctx % 2 * half + ctx // 2) * WIDTH).astype(jnp.int32).reshape(1)

    spread = pl.pallas_call(
        spread_kernel,
        grid=(2,),
        in_specs=[pl.BlockSpec((width_dev // 2, span), lambda k: (k, 0))] * 2,
        out_specs=pl.BlockSpec((half, 1, 2, WIDTH, ROWS, R), lambda k: (0, k, 0, 0, 0, 0)),
        out_shape=jax.ShapeDtypeStruct((half, 2, 2, WIDTH, ROWS, R), F32),
        name="spread",
    )(prompt_input, filters)
    spread = spread.reshape(ctx_count, 2, WIDTH, ROWS, R)
    regrouped = lax.all_to_all(spread, "ctx", split_axis=0, concat_axis=0, tiled=True)

    consts = [jnp.asarray(table) for table in tables()]
    consts = consts
    consts = pl.pallas_call(
        hold_kernel,
        in_specs=[ANY] * (1 + len(consts)),
        out_specs=[VMEM] * len(consts),
        out_shape=[jax.ShapeDtypeStruct(table.shape, table.dtype) for table in consts],
        scratch_shapes=[pltpu.SemaphoreType.DMA((len(consts),))],
        compiler_params=pltpu.CompilerParams(vmem_limit_bytes=40 * 2**20),
        name="hold",
    )(spread, *consts)
    consts, holds = consts[:5], consts[5:]
    convolved, tail = pl.pallas_call(
        conv_kernel,
        in_specs=[SMEM, ANY, VMEM, ANY] + [VMEM] * 5 + [ANY] * len(holds),
        out_specs=[ANY, VMEM],
        out_shape=[
            jax.ShapeDtypeStruct((ctx_count, WIDTH, ROWS, R), F32),
            jax.ShapeDtypeStruct((ROWS, WIDTH, R), F32),
        ],
        scratch_shapes=[
            pltpu.SMEM(skip.shape, F32),
            pltpu.VMEM((ctx_count, WIDTH, ROWS, R), F32),
            pltpu.SemaphoreType.DMA,
            pltpu.SemaphoreType.DMA,
        ],
        compiler_params=pltpu.CompilerParams(vmem_limit_bytes=30 * 2**20),
        name="conv",
    )(base, place, regrouped, skip, *consts, *holds)

    tail = tail[None]
    held = jnp.concatenate([tail] + [take_from(tail, o) for o in FIRST], 0)
    held = jnp.concatenate([held] + [take_from(held, o) for o in SECOND], 0)
    mine = [held] + [take_from(held, o, mirrored=True) for o in THIRD]
    other = [swap_cores(part) for part in mine]

    local, length, channels = sample_input.shape
    block = pl.BlockSpec((local, R, channels), lambda j: (0, j, 0))
    sample_output, done = pl.pallas_call(
        sample_kernel,
        grid=(length // R,),
        in_specs=[SMEM, SMEM, pl.BlockSpec((1, channels), lambda j: (0, 0)), block, block] + [ANY] * 8,
        out_specs=[block, pl.BlockSpec((8, R), lambda j: (0, 0))],
        out_shape=[jax.ShapeDtypeStruct(sample_input.shape, BF16), jax.ShapeDtypeStruct((8, R), F32)],
        scratch_shapes=[pltpu.VMEM((ROWS, channels, R), F32), pltpu.SemaphoreType.DMA],
        compiler_params=pltpu.CompilerParams(vmem_limit_bytes=50 * 2**20),
        name="samples",
    )(place, lengths, skip.reshape(1, channels), sample_input, sample_gate, *mine, *other)

    returned = lax.all_to_all(convolved, "ctx", split_axis=0, concat_axis=0, tiled=True)
    prompt_output = pl.pallas_call(
        finish_kernel,
        grid=(2,),
        in_specs=[
            ANY,
            pl.BlockSpec((half, 1, WIDTH, ROWS, R), lambda k: (0, k, 0, 0, 0)),
            pl.BlockSpec((width_dev // 2, span), lambda k: (k, 0)),
        ],
        out_specs=pl.BlockSpec((width_dev // 2, span), lambda k: (k, 0)),
        out_shape=jax.ShapeDtypeStruct((width_dev, span), BF16),
        name="finish",
    )(done, returned.reshape(half, 2, WIDTH, ROWS, R), prompt_gate)
    return prompt_output, sample_output


def solution(mesh):
    return jax.shard_map(
        on_device,
        mesh=mesh,
        in_specs=(
            P("smp", "ctx"),
            P("smp", "ctx"),
            P("smp", "ctx"),
            P(),
            P(("ctx", "smp"), None, None),
            P(("ctx", "smp"), None, None),
            P(("ctx", "smp")),
        ),
        out_specs=(P("smp", "ctx"), P(("ctx", "smp"), None, None)),
        check_vma=False,
    )
```

```python
import functools

import jax
import jax.numpy as jnp
import numpy as np
from jax import lax
from jax.experimental import pallas as pl
from jax.experimental.pallas import tpu as pltpu
from jax.sharding import PartitionSpec as P

F32 = jnp.float32
BF16 = jnp.bfloat16
R = 128
ROWS = 8
SIDE = 4
AXES = ("ctx", "smp")

FIRST = ((1, 1, 1), (2, 2, 2), (3, 3, 3))
SECOND = ((2, 0, 0), (0, 2, 0), (0, 0, 2))
THIRD = ((0, 1, 0), (0, 0, 1), (1, 0, 0))
HELD_FIRST = ((0, 0, 0),) + FIRST
HELD_SECOND = tuple(
    tuple((a + b) % SIDE for a, b in zip(o, h)) for o in ((0, 0, 0),) + SECOND for h in HELD_FIRST
)


def chip_of(index):
    ctx, smp = divmod(index, 8)
    return ((ctx >> 1 & 1) * 2 + (smp & 1), ctx >> 2, smp >> 1, ctx & 1)


def index_of(x, y, z, core):
    x, y, z = x % SIDE, y % SIDE, z % SIDE
    return ((y * 2 + x // 2) * 2 + core) * 8 + z * 2 + x % 2


def over_ctx(array):
    groups = [[((slot % 8) * 2 + slot // 8) * 8 + smp for slot in range(16)] for smp in range(8)]
    return lax.all_to_all(array, AXES, split_axis=0, concat_axis=0, tiled=True, axis_index_groups=groups)


def take_from(array, offset, mirrored=False):
    pairs = []
    for index in range(2 * SIDE**3):
        x, y, z, core = chip_of(index)
        sign = -1 if mirrored and core else 1
        source = index_of(x + sign * offset[0], y + sign * offset[1], z + sign * offset[2], core)
        pairs.append((source, index))
    return lax.ppermute(array, AXES, pairs)


def swap_cores(array):
    pairs = []
    for index in range(2 * SIDE**3):
        x, y, z, core = chip_of(index)
        pairs.append((index, index_of(x, y, z, 1 - core)))
    return lax.ppermute(array, AXES, pairs)


def halves(values):
    high = values.astype(BF16)
    return high, (values - high.astype(F32)).astype(BF16)


def np_halves(values):
    values = np.asarray(values, np.float32)
    high = values.astype(jnp.bfloat16)
    low = (values - high.astype(np.float32)).astype(jnp.bfloat16)
    return high, low


@functools.cache
def tables():
    period = R * R
    r = np.arange(R)
    shifted = r + 0.25
    rows = np.concatenate([((slot % 8) * 2 + slot // 8) * ROWS + np.arange(ROWS) for slot in range(16)])
    outer = 2 * np.pi * np.outer(shifted, rows) / R
    first = np.concatenate([np.cos(outer), -np.sin(outer)], 0)
    inner = 2 * np.pi * (np.outer(r, r) % R) / R
    c, s = np.cos(inner), np.sin(inner)
    second = np.block([[c, -s], [s, c]])
    back = np.block([[c, s], [-s, c]])
    twist = 2 * np.pi * np.outer(shifted, r) / period
    turn = np.stack([np.cos(twist), np.sin(twist)]).astype(np.float32)
    real = np.concatenate([np.cos(outer.T), -np.sin(outer.T)], 1)
    leading = 2 * np.pi * np.outer(r[:ROWS], shifted) / R
    tail = -np.concatenate([np.sin(leading), np.cos(leading)], 1)
    last = np.concatenate([real, tail, np.zeros((ROWS, 2 * R))], 0)
    f_hi, f_lo = np_halves(first)
    l_hi, l_lo = np_halves(last / period)
    return (
        np.concatenate([f_hi, f_lo], 1),
        np.stack(np_halves(second)),
        np.stack(np_halves(back)),
        np.stack([l_hi, l_lo]),
        turn,
    )


@functools.cache
def arrivals():
    table = np.zeros((2 * SIDE**3, 8 * 16), np.int32)
    for index in range(2 * SIDE**3):
        own = chip_of(index)
        for array in range(8):
            core = own[3] ^ (array // 4)
            extra = ((0, 0, 0),) + THIRD
            for slot, held in enumerate(HELD_SECOND):
                sign = -1 if core else 1
                x, y, z = [(own[i] + held[i] + sign * extra[array % 4][i]) % SIDE for i in range(3)]
                table[index, array * 16 + slot] = (z * 2 + x % 2) * 256 + core * 128 + (y * 2 + x // 2) * 16
    return table


def dot(left, right):
    return jnp.dot(left, right, preferred_element_type=F32)


WIDTH = 16
GROUP = 2


def spread_kernel(signal_ref, filter_ref, out_ref):
    for k in range(out_ref.shape[0]):
        rows = pl.ds(k * WIDTH, WIDTH)
        out_ref[k, 0] = signal_ref[rows, :].astype(F32).reshape(WIDTH, ROWS, R)
        out_ref[k, 1] = filter_ref[rows, :].reshape(WIDTH, ROWS, R)


def conv_kernel(base_ref, place_ref, in_ref, skip_hbm, *refs):
    first_ref, second_ref, back_ref, last_ref, turn_ref = refs[:5]
    out_hbm, tail_ref, skip_ref, out_ref, skip_sem, out_sem = refs[-6:]
    ctx_count = in_ref.shape[0]
    parts = in_ref.shape[2] // GROUP
    load = pltpu.make_async_copy(skip_hbm, skip_ref, skip_sem)
    load.start()
    f_both = first_ref[...]
    f_hi = first_ref[:, :R]

    def chans(part):
        return [part * GROUP + k for k in range(GROUP)]

    def columns(part):
        signal = [in_ref[:, 0, c].reshape(R, R) for c in chans(part)]
        taps = [in_ref[:, 1, c].reshape(R, R) for c in chans(part)]
        x = jnp.concatenate(signal, 1).astype(BF16)
        h_hi, h_lo = halves(jnp.concatenate(taps, 1))
        xs = dot(f_both, jnp.concatenate([x, x], 0))
        hs = dot(f_both, jnp.concatenate([h_hi, h_hi], 0)) + dot(f_hi, h_lo)
        cos, sin = turn_ref[0], turn_ref[1]
        rows = []
        for spec in (xs, hs):
            for k in range(GROUP):
                re, im = spec[:R, k * R : (k + 1) * R], spec[R:, k * R : (k + 1) * R]
                rows.append(jnp.concatenate([re * cos + im * sin, im * cos - re * sin], 1))
        return halves(jnp.concatenate(rows, 0))

    def product(part, value):
        hi, lo = value
        spectra = dot(hi, second_ref[0]) + dot(lo, second_ref[0]) + dot(hi, second_ref[1])
        prods = []
        for k in range(GROUP):
            xr, xi = spectra[k * R : (k + 1) * R, :R], spectra[k * R : (k + 1) * R, R:]
            other = GROUP + k
            hr, hq = spectra[other * R : (other + 1) * R, :R], spectra[other * R : (other + 1) * R, R:]
            prods.append(jnp.concatenate([xr * hr - xi * hq, xr * hq + xi * hr], 1))
        return halves(jnp.concatenate(prods, 0))

    def returning(part, value):
        hi, lo = value
        timed = dot(hi, back_ref[0]) + dot(lo, back_ref[0]) + dot(hi, back_ref[1])
        cos, sin = turn_ref[0], turn_ref[1]
        cols = []
        for k in range(GROUP):
            re, im = timed[k * R : (k + 1) * R, :R], timed[k * R : (k + 1) * R, R:]
            cols.append(jnp.concatenate([re * cos - im * sin, re * sin + im * cos], 0))
        return halves(jnp.concatenate(cols, 1))

    def positions(part, value):
        hi, lo = value
        result = dot(last_ref[0], hi) + dot(last_ref[0], lo) + dot(last_ref[1], hi)
        for k, c in enumerate(chans(part)):
            conv = result[:R, k * R : (k + 1) * R] + skip_ref[base_ref[0] + c] * in_ref[:, 0, c].reshape(R, R)
            out_ref[:, c] = conv.reshape(ctx_count, ROWS, R)
            tail_ref[:, c, :] = result[R : R + ROWS, k * R : (k + 1) * R]

    values = {}
    for step in range(parts + 3):
        for stage, section in ((3, positions), (2, returning), (1, product), (0, columns)):
            part = step - stage
            if stage == 3 and part == 0:
                load.wait()
            if 0 <= part < parts:
                values[part] = section(part, values[part]) if stage else section(part)
    leave = pltpu.make_async_copy(out_ref, out_hbm, out_sem)
    leave.start()
    leave.wait()


def finish_kernel(after_ref, conv_ref, gate_ref, out_ref):
    for k in range(conv_ref.shape[0]):
        rows = pl.ds(k * WIDTH, WIDTH)
        conv = conv_ref[k].reshape(WIDTH, ROWS * R)
        out_ref[rows, :] = (gate_ref[rows, :].astype(F32) * conv).astype(BF16)


def hold_kernel(after_ref, *refs):
    count = len(refs) // 2
    copies = [pltpu.make_async_copy(refs[i], refs[count + i], refs[-1].at[i]) for i in range(count)]
    for copy in copies:
        copy.start()
    for copy in copies:
        copy.wait()


def sample_kernel(place_ref, lengths_ref, skip_ref, input_ref, gate_ref, *rest):
    pieces, (out_ref, done_ref, tail_ref, sem) = rest[:8], rest[8:]
    step = pl.program_id(0)

    @pl.when(step == 0)
    def _():
        done_ref[...] = jnp.zeros_like(done_ref)
        for array, piece_ref in enumerate(pieces):
            for slot in range(16):
                channel = pl.multiple_of(place_ref[array * 16 + slot], WIDTH)
                pltpu.make_async_copy(piece_ref.at[slot], tail_ref.at[:, pl.ds(channel, WIDTH)], sem).start()
        pltpu.make_async_copy(tail_ref, tail_ref, sem).wait()

    positions = step * R + lax.broadcasted_iota(jnp.int32, (R, R), 0)
    for block in range(tail_ref.shape[1] // R):
        cols = pl.ds(block * R, R)
        state = tail_ref[step, cols, :].T
        for i in range(input_ref.shape[0]):
            blended = gate_ref[i, :, cols].astype(F32) * (
                state + skip_ref[:, cols] * input_ref[i, :, cols].astype(F32)
            )
            out_ref[i, :, cols] = jnp.where(positions < lengths_ref[i], blended, 0.0).astype(BF16)


VMEM = pl.BlockSpec(memory_space=pltpu.VMEM)
SMEM = pl.BlockSpec(memory_space=pltpu.SMEM)
ANY = pl.BlockSpec(memory_space=pl.ANY)


def on_device(prompt_input, prompt_gate, filters, skip, sample_input, sample_gate, lengths):
    width_dev, span = prompt_input.shape
    ctx_count = 16
    half = ctx_count // 2
    ctx, smp = lax.axis_index("ctx"), lax.axis_index("smp")
    place = lax.dynamic_index_in_dim(jnp.asarray(arrivals()), ctx * 8 + smp, keepdims=False)
    base = (smp * width_dev + (ctx % 2 * half + ctx // 2) * WIDTH).astype(jnp.int32).reshape(1)

    spread = pl.pallas_call(
        spread_kernel,
        grid=(2,),
        in_specs=[pl.BlockSpec((width_dev // 2, span), lambda k: (k, 0))] * 2,
        out_specs=pl.BlockSpec((half, 2, WIDTH, ROWS, R), lambda k: (k, 0, 0, 0, 0)),
        out_shape=jax.ShapeDtypeStruct((ctx_count, 2, WIDTH, ROWS, R), F32),
        name="spread",
    )(prompt_input, filters)
    regrouped = over_ctx(spread)

    consts = [jnp.asarray(table) for table in tables()]
    consts = consts
    consts = pl.pallas_call(
        hold_kernel,
        in_specs=[ANY] * (1 + len(consts)),
        out_specs=[VMEM] * len(consts),
        out_shape=[jax.ShapeDtypeStruct(table.shape, table.dtype) for table in consts],
        scratch_shapes=[pltpu.SemaphoreType.DMA((len(consts),))],
        compiler_params=pltpu.CompilerParams(vmem_limit_bytes=40 * 2**20),
        name="hold",
    )(spread, *consts)
    consts, holds = consts[:5], consts[5:]
    convolved, tail = pl.pallas_call(
        conv_kernel,
        in_specs=[SMEM, ANY, VMEM, ANY] + [VMEM] * 5 + [ANY] * len(holds),
        out_specs=[ANY, VMEM],
        out_shape=[
            jax.ShapeDtypeStruct((ctx_count, WIDTH, ROWS, R), F32),
            jax.ShapeDtypeStruct((ROWS, WIDTH, R), F32),
        ],
        scratch_shapes=[
            pltpu.SMEM(skip.shape, F32),
            pltpu.VMEM((ctx_count, WIDTH, ROWS, R), F32),
            pltpu.SemaphoreType.DMA,
            pltpu.SemaphoreType.DMA,
        ],
        compiler_params=pltpu.CompilerParams(vmem_limit_bytes=30 * 2**20),
        name="conv",
    )(base, place, regrouped, skip, *consts, *holds)

    tail = tail[None]
    held = jnp.concatenate([tail] + [take_from(tail, o) for o in FIRST], 0)
    held = jnp.concatenate([held] + [take_from(held, o) for o in SECOND], 0)
    mine = [held] + [take_from(held, o, mirrored=True) for o in THIRD]
    other = [swap_cores(part) for part in mine]

    local, length, channels = sample_input.shape
    block = pl.BlockSpec((local, R, channels), lambda j: (0, j, 0))
    sample_output, done = pl.pallas_call(
        sample_kernel,
        grid=(length // R,),
        in_specs=[SMEM, SMEM, pl.BlockSpec((1, channels), lambda j: (0, 0)), block, block] + [ANY] * 8,
        out_specs=[block, pl.BlockSpec((8, R), lambda j: (0, 0))],
        out_shape=[jax.ShapeDtypeStruct(sample_input.shape, BF16), jax.ShapeDtypeStruct((8, R), F32)],
        scratch_shapes=[pltpu.VMEM((ROWS, channels, R), F32), pltpu.SemaphoreType.DMA],
        compiler_params=pltpu.CompilerParams(vmem_limit_bytes=50 * 2**20),
        name="samples",
    )(place, lengths, skip.reshape(1, channels), sample_input, sample_gate, *mine, *other)

    returned = over_ctx(convolved)
    prompt_output = pl.pallas_call(
        finish_kernel,
        grid=(2,),
        in_specs=[
            ANY,
            pl.BlockSpec((half, WIDTH, ROWS, R), lambda k: (k, 0, 0, 0)),
            pl.BlockSpec((width_dev // 2, span), lambda k: (k, 0)),
        ],
        out_specs=pl.BlockSpec((width_dev // 2, span), lambda k: (k, 0)),
        out_shape=jax.ShapeDtypeStruct((width_dev, span), BF16),
        name="finish",
    )(done, returned, prompt_gate)
    return prompt_output, sample_output


def solution(mesh):
    return jax.shard_map(
        on_device,
        mesh=mesh,
        in_specs=(
            P("smp", "ctx"),
            P("smp", "ctx"),
            P("smp", "ctx"),
            P(),
            P(("ctx", "smp"), None, None),
            P(("ctx", "smp"), None, None),
            P(("ctx", "smp")),
        ),
        out_specs=(P("smp", "ctx"), P(("ctx", "smp"), None, None)),
        check_vma=False,
    )
```

```python
import functools

import jax
import jax.numpy as jnp
import numpy as np
from jax import lax
from jax.experimental import pallas as pl
from jax.experimental.pallas import tpu as pltpu
from jax.sharding import PartitionSpec as P

F32 = jnp.float32
BF16 = jnp.bfloat16
R = 128
ROWS = 8
SIDE = 4
AXES = ("ctx", "smp")

FIRST = ((1, 1, 1), (2, 2, 2), (3, 3, 3))
SECOND = ((2, 0, 0), (0, 2, 0), (0, 0, 2))
THIRD = ((0, 1, 0), (0, 0, 1), (1, 0, 0))
HELD_FIRST = ((0, 0, 0),) + FIRST
HELD_SECOND = tuple(
    tuple((a + b) % SIDE for a, b in zip(o, h)) for o in ((0, 0, 0),) + SECOND for h in HELD_FIRST
)


def chip_of(index):
    ctx, smp = divmod(index, 8)
    return ((ctx >> 1 & 1) * 2 + (smp & 1), ctx >> 2, smp >> 1, ctx & 1)


def index_of(x, y, z, core):
    x, y, z = x % SIDE, y % SIDE, z % SIDE
    return ((y * 2 + x // 2) * 2 + core) * 8 + z * 2 + x % 2


def over_ctx(array):
    groups = [[((slot % 8) * 2 + slot // 8) * 8 + smp for slot in range(16)] for smp in range(8)]
    return lax.all_to_all(array, AXES, split_axis=0, concat_axis=0, tiled=True, axis_index_groups=groups)


def take_from(array, offset, mirrored=False):
    pairs = []
    for index in range(2 * SIDE**3):
        x, y, z, core = chip_of(index)
        sign = -1 if mirrored and core else 1
        source = index_of(x + sign * offset[0], y + sign * offset[1], z + sign * offset[2], core)
        pairs.append((source, index))
    return lax.ppermute(array, AXES, pairs)


def swap_cores(array):
    pairs = []
    for index in range(2 * SIDE**3):
        x, y, z, core = chip_of(index)
        pairs.append((index, index_of(x, y, z, 1 - core)))
    return lax.ppermute(array, AXES, pairs)


def halves(values):
    high = values.astype(BF16)
    return high, (values - high.astype(F32)).astype(BF16)


def np_halves(values):
    values = np.asarray(values, np.float32)
    high = values.astype(jnp.bfloat16)
    low = (values - high.astype(np.float32)).astype(jnp.bfloat16)
    return high, low


@functools.cache
def tables():
    period = R * R
    r = np.arange(R)
    shifted = r + 0.25
    rows = np.concatenate([((slot % 8) * 2 + slot // 8) * ROWS + np.arange(ROWS) for slot in range(16)])
    outer = 2 * np.pi * np.outer(shifted, rows) / R
    first = np.concatenate([np.cos(outer), -np.sin(outer)], 0)
    inner = 2 * np.pi * (np.outer(r, r) % R) / R
    c, s = np.cos(inner), np.sin(inner)
    second = np.block([[c, -s], [s, c]])
    back = np.block([[c, s], [-s, c]])
    twist = 2 * np.pi * np.outer(shifted, r) / period
    turn = np.stack([np.cos(twist), np.sin(twist)]).astype(np.float32)
    real = np.concatenate([np.cos(outer.T), -np.sin(outer.T)], 1)
    leading = 2 * np.pi * np.outer(r[:ROWS], shifted) / R
    tail = -np.concatenate([np.sin(leading), np.cos(leading)], 1)
    last = np.concatenate([real, tail, np.zeros((ROWS, 2 * R))], 0)
    f_hi, f_lo = np_halves(first)
    l_hi, l_lo = np_halves(last / period)
    return (
        np.concatenate([f_hi, f_lo], 1),
        np.stack(np_halves(second)),
        np.stack(np_halves(back)),
        np.stack([l_hi, l_lo]),
        turn,
    )


@functools.cache
def arrivals():
    table = np.zeros((2 * SIDE**3, 8 * 16), np.int32)
    for index in range(2 * SIDE**3):
        own = chip_of(index)
        for array in range(8):
            core = own[3] ^ (array // 4)
            extra = ((0, 0, 0),) + THIRD
            for slot, held in enumerate(HELD_SECOND):
                sign = -1 if core else 1
                x, y, z = [(own[i] + held[i] + sign * extra[array % 4][i]) % SIDE for i in range(3)]
                table[index, array * 16 + slot] = (z * 2 + x % 2) * 256 + core * 128 + (y * 2 + x // 2) * 16
    return table


def dot(left, right):
    return jnp.dot(left, right, preferred_element_type=F32)


WIDTH = 16
GROUP = 2


def spread_kernel(signal_ref, filter_ref, out_ref):
    for k in range(out_ref.shape[0]):
        rows = pl.ds(k * WIDTH, WIDTH)
        out_ref[k, 0] = signal_ref[rows, :].astype(F32).reshape(WIDTH, ROWS, R)
        out_ref[k, 1] = filter_ref[rows, :].reshape(WIDTH, ROWS, R)


def conv_kernel(base_ref, place_ref, in_ref, skip_hbm, *refs):
    first_ref, second_ref, back_ref, last_ref, turn_ref = refs[:5]
    out_hbm, tail_ref, skip_ref, out_ref, skip_sem, out_sem = refs[-6:]
    ctx_count = in_ref.shape[0]
    parts = in_ref.shape[2] // GROUP
    load = pltpu.make_async_copy(skip_hbm, skip_ref, skip_sem)
    load.start()
    f_both = first_ref[...]
    f_hi = first_ref[:, :R]

    def chans(part):
        return [part * GROUP + k for k in range(GROUP)]

    def columns(part):
        signal = [in_ref[:, 0, c].reshape(R, R) for c in chans(part)]
        taps = [in_ref[:, 1, c].reshape(R, R) for c in chans(part)]
        x = jnp.concatenate(signal, 1).astype(BF16)
        h_hi, h_lo = halves(jnp.concatenate(taps, 1))
        xs = dot(f_both, jnp.concatenate([x, x], 0))
        hs = dot(f_both, jnp.concatenate([h_hi, h_hi], 0)) + dot(f_hi, h_lo)
        cos, sin = turn_ref[0], turn_ref[1]
        rows = []
        for spec in (xs, hs):
            for k in range(GROUP):
                re, im = spec[:R, k * R : (k + 1) * R], spec[R:, k * R : (k + 1) * R]
                rows.append(jnp.concatenate([re * cos + im * sin, im * cos - re * sin], 1))
        return halves(jnp.concatenate(rows, 0))

    def product(part, value):
        hi, lo = value
        spectra = dot(hi, second_ref[0]) + dot(lo, second_ref[0]) + dot(hi, second_ref[1])
        prods = []
        for k in range(GROUP):
            xr, xi = spectra[k * R : (k + 1) * R, :R], spectra[k * R : (k + 1) * R, R:]
            other = GROUP + k
            hr, hq = spectra[other * R : (other + 1) * R, :R], spectra[other * R : (other + 1) * R, R:]
            prods.append(jnp.concatenate([xr * hr - xi * hq, xr * hq + xi * hr], 1))
        return halves(jnp.concatenate(prods, 0))

    def returning(part, value):
        hi, lo = value
        timed = dot(hi, back_ref[0]) + dot(lo, back_ref[0]) + dot(hi, back_ref[1])
        cos, sin = turn_ref[0], turn_ref[1]
        cols = []
        for k in range(GROUP):
            re, im = timed[k * R : (k + 1) * R, :R], timed[k * R : (k + 1) * R, R:]
            cols.append(jnp.concatenate([re * cos - im * sin, re * sin + im * cos], 0))
        return halves(jnp.concatenate(cols, 1))

    def positions(part, value):
        hi, lo = value
        result = dot(last_ref[0], hi) + dot(last_ref[0], lo) + dot(last_ref[1], hi)
        for k, c in enumerate(chans(part)):
            conv = result[:R, k * R : (k + 1) * R] + skip_ref[base_ref[0] + c] * in_ref[:, 0, c].reshape(R, R)
            out_ref[:, c] = conv.reshape(ctx_count, ROWS, R)
            tail_ref[:, c, :] = result[R : R + ROWS, k * R : (k + 1) * R]

    values = {}
    for step in range(parts + 3):
        for stage, section in ((3, positions), (2, returning), (1, product), (0, columns)):
            part = step - stage
            if stage == 3 and part == 0:
                load.wait()
            if 0 <= part < parts:
                values[part] = section(part, values[part]) if stage else section(part)
    leave = pltpu.make_async_copy(out_ref, out_hbm, out_sem)
    leave.start()
    leave.wait()


def finish_kernel(after_ref, conv_ref, gate_ref, out_ref):
    for k in range(conv_ref.shape[0]):
        rows = pl.ds(k * WIDTH, WIDTH)
        conv = conv_ref[k].reshape(WIDTH, ROWS * R)
        out_ref[rows, :] = (gate_ref[rows, :].astype(F32) * conv).astype(BF16)


def hold_kernel(after_ref, *refs):
    count = len(refs) // 2
    copies = [pltpu.make_async_copy(refs[i], refs[count + i], refs[-1].at[i]) for i in range(count)]
    for copy in copies:
        copy.start()
    for copy in copies:
        copy.wait()


def sample_kernel(place_ref, lengths_ref, skip_ref, input_hbm, gate_hbm, *rest):
    pieces, (out_hbm, tail_ref, input_ref, gate_ref, out_ref, tail_sem, in_sem, out_sem) = rest[:8], rest[8:]
    steps = input_ref.shape[1] // R

    def fetches(step, i):
        rows = pl.ds(pl.multiple_of(step * R, R), R)
        return [
            pltpu.make_async_copy(input_hbm.at[i, rows], input_ref.at[i, rows], in_sem.at[step, i, 0]),
            pltpu.make_async_copy(gate_hbm.at[i, rows], gate_ref.at[i, rows], in_sem.at[step, i, 1]),
        ]

    for array, piece_ref in enumerate(pieces):
        for slot in range(16):
            channel = pl.multiple_of(place_ref[array * 16 + slot], WIDTH)
            pltpu.make_async_copy(piece_ref.at[slot], tail_ref.at[:, pl.ds(channel, WIDTH)], tail_sem).start()
    for step in range(steps):
        for i in range(input_ref.shape[0]):
            for fetch in fetches(step, i):
                fetch.start()
    pltpu.make_async_copy(tail_ref, tail_ref, tail_sem).wait()

    def rows_of(step, carry):
        here = pl.ds(pl.multiple_of(step * R, R), R)
        positions = step * R + lax.broadcasted_iota(jnp.int32, (R, R), 0)
        for i in range(input_ref.shape[0]):
            for fetch in fetches(step, i):
                fetch.wait()
        for block in range(tail_ref.shape[1] // R):
            cols = pl.ds(block * R, R)
            state = tail_ref[step, cols, :].T
            for i in range(input_ref.shape[0]):
                blended = gate_ref[i, here, cols].astype(F32) * (
                    state + skip_ref[:, cols] * input_ref[i, here, cols].astype(F32)
                )
                out_ref[i, here, cols] = jnp.where(positions < lengths_ref[i], blended, 0.0).astype(BF16)
        for i in range(input_ref.shape[0]):
            pltpu.make_async_copy(out_ref.at[i, here], out_hbm.at[i, here], out_sem).start()
        return carry

    lax.fori_loop(0, steps, rows_of, 0)
    pltpu.make_async_copy(out_ref, out_hbm, out_sem).wait()


VMEM = pl.BlockSpec(memory_space=pltpu.VMEM)
SMEM = pl.BlockSpec(memory_space=pltpu.SMEM)
ANY = pl.BlockSpec(memory_space=pl.ANY)


def on_device(prompt_input, prompt_gate, filters, skip, sample_input, sample_gate, lengths):
    width_dev, span = prompt_input.shape
    ctx_count = 16
    half = ctx_count // 2
    ctx, smp = lax.axis_index("ctx"), lax.axis_index("smp")
    place = lax.dynamic_index_in_dim(jnp.asarray(arrivals()), ctx * 8 + smp, keepdims=False)
    base = (smp * width_dev + (ctx % 2 * half + ctx // 2) * WIDTH).astype(jnp.int32).reshape(1)

    spread = pl.pallas_call(
        spread_kernel,
        grid=(2,),
        in_specs=[pl.BlockSpec((width_dev // 2, span), lambda k: (k, 0))] * 2,
        out_specs=pl.BlockSpec((half, 2, WIDTH, ROWS, R), lambda k: (k, 0, 0, 0, 0)),
        out_shape=jax.ShapeDtypeStruct((ctx_count, 2, WIDTH, ROWS, R), F32),
        name="spread",
    )(prompt_input, filters)
    regrouped = over_ctx(spread)

    consts = [jnp.asarray(table) for table in tables()]
    consts = consts
    consts = pl.pallas_call(
        hold_kernel,
        in_specs=[ANY] * (1 + len(consts)),
        out_specs=[VMEM] * len(consts),
        out_shape=[jax.ShapeDtypeStruct(table.shape, table.dtype) for table in consts],
        scratch_shapes=[pltpu.SemaphoreType.DMA((len(consts),))],
        compiler_params=pltpu.CompilerParams(vmem_limit_bytes=40 * 2**20),
        name="hold",
    )(spread, *consts)
    consts, holds = consts[:5], consts[5:]
    convolved, tail = pl.pallas_call(
        conv_kernel,
        in_specs=[SMEM, ANY, VMEM, ANY] + [VMEM] * 5 + [ANY] * len(holds),
        out_specs=[ANY, VMEM],
        out_shape=[
            jax.ShapeDtypeStruct((ctx_count, WIDTH, ROWS, R), F32),
            jax.ShapeDtypeStruct((ROWS, WIDTH, R), F32),
        ],
        scratch_shapes=[
            pltpu.SMEM(skip.shape, F32),
            pltpu.VMEM((ctx_count, WIDTH, ROWS, R), F32),
            pltpu.SemaphoreType.DMA,
            pltpu.SemaphoreType.DMA,
        ],
        compiler_params=pltpu.CompilerParams(vmem_limit_bytes=30 * 2**20),
        name="conv",
    )(base, place, regrouped, skip, *consts, *holds)

    tail = tail[None]
    held = jnp.concatenate([tail] + [take_from(tail, o) for o in FIRST], 0)
    held = jnp.concatenate([held] + [take_from(held, o) for o in SECOND], 0)
    mine = [held] + [take_from(held, o, mirrored=True) for o in THIRD]
    other = [swap_cores(part) for part in mine]

    local, length, channels = sample_input.shape
    sample_output = pl.pallas_call(
        sample_kernel,
        in_specs=[SMEM, SMEM, VMEM, ANY, ANY] + [ANY] * 8,
        out_specs=ANY,
        out_shape=jax.ShapeDtypeStruct(sample_input.shape, BF16),
        scratch_shapes=[
            pltpu.VMEM((ROWS, channels, R), F32),
            *[pltpu.VMEM(sample_input.shape, BF16)] * 3,
            pltpu.SemaphoreType.DMA,
            pltpu.SemaphoreType.DMA((length // R, local, 2)),
            pltpu.SemaphoreType.DMA,
        ],
        compiler_params=pltpu.CompilerParams(vmem_limit_bytes=50 * 2**20),
        name="samples",
    )(place, lengths, skip.reshape(1, channels), sample_input, sample_gate, *mine, *other)

    returned = over_ctx(convolved)
    prompt_output = pl.pallas_call(
        finish_kernel,
        grid=(2,),
        in_specs=[
            ANY,
            pl.BlockSpec((half, WIDTH, ROWS, R), lambda k: (k, 0, 0, 0)),
            pl.BlockSpec((width_dev // 2, span), lambda k: (k, 0)),
        ],
        out_specs=pl.BlockSpec((width_dev // 2, span), lambda k: (k, 0)),
        out_shape=jax.ShapeDtypeStruct((width_dev, span), BF16),
        name="finish",
    )(sample_output, returned, prompt_gate)
    return prompt_output, sample_output


def solution(mesh):
    return jax.shard_map(
        on_device,
        mesh=mesh,
        in_specs=(
            P("smp", "ctx"),
            P("smp", "ctx"),
            P("smp", "ctx"),
            P(),
            P(("ctx", "smp"), None, None),
            P(("ctx", "smp"), None, None),
            P(("ctx", "smp")),
        ),
        out_specs=(P("smp", "ctx"), P(("ctx", "smp"), None, None)),
        check_vma=False,
    )
```
